32 devices in a mesh: groups: 2 (over y), rows: 8 (over z, x), cols: 2 (over core).
Axes of the slice: x: 2, y: 2, z: 4, core: 2. Of those that a mesh axis runs over, the one named last changes fastest.
Arguments:
- features: bfloat16 [64, 4096], P(('groups', 'rows'), 'cols'), parts along dimension 0, may hold values from -6 to 6
- weights: bfloat16 [4, 2, 8, 6, 256, 256], P(None, 'cols', 'rows'), may hold values from -0.25 to 0.25
- active: int32 [4, 2, 8, 6], P(None, 'cols', 'rows'), may hold values 0 or 1
- layer_bias: float32 [4, 2, 8, 256], P(None, 'cols', 'rows'), may hold values from -0.5 to 0.3
Outputs:
- activations: bfloat16 [64, 4096], P(('groups', 'rows'), 'cols'), parts along dimension 0
The draws below stay inside these ranges and needn't reach their ends.
There are 2 independent parts, one for each index of `groups`. The reference program is written for one: setup_inputs(seed, part) draws one part's arguments, and reference() takes and returns one part's arrays. A program takes and returns all parts, laid end to end along the dimension named above; an argument that names none is the same for every part. Nothing has to cross between parts.
Inputs may be any that keep to these rules, and one draw needn't show every extreme that they name: `active`: 1 marks a source block that feeds the output block.
All inputs are finite; a program needn't handle non-finite values.
Results may differ from the reference program's by a relative error of at most 0.0066.
Values may be sent and summed in bfloat16 or wider, within the bound.
No kernel may reach another device: no remote copies, remote signals or barrier semaphores. Data moves between devices by JAX's collectives and lax.ppermute only.
A program may use at most 64 MiB of HBM per device.

```python
import jax
import jax.numpy as jnp

BLOCK = 256
REACH = 2
CAND = 6
LAYER_TOTAL = 4
NBH = 8
NEURONS = 4096
ROWS = 32


def plant(array, rng, low, largest):
    extent = array.shape
    place = [jax.random.randint(jax.random.fold_in(rng, axis), (), 0, extent[axis]) for axis in range(len(extent))]
    array = array.at[tuple(place)].set(low)
    longest = extent.index(max(extent))
    place[longest] = (place[longest] + 1) % extent[longest]
    return array.at[tuple(place)].set(largest)


def steps_of(stream_key, extent, shards, least, high):
    loudness = 1.0
    for dim, parts in shards:
        steps = jax.random.uniform(jax.random.fold_in(jax.random.fold_in(stream_key, 6), dim), (parts,), jnp.float32, least / len(shards), high / len(shards))
        loudness = loudness * jnp.repeat(jnp.exp(steps), extent[dim] // parts).reshape((-1,) + (1,) * (len(extent) - 1 - dim))
    return loudness


def bell_draw(key, dims, deviation, bound, pieces=(), dtype=jnp.bfloat16):
    gain = steps_of(key, dims, pieces, -0.22, 0.18) if pieces else 1.0
    values = jax.random.normal(key, dims, jnp.float32) * deviation * gain
    return jnp.minimum(jnp.maximum(values, -bound), bound).astype(dtype)


def setup_inputs(seed: int = 0, part: int = 0) -> dict:
    seeds = jax.random.split(jax.random.key(seed), 5)
    own_keys = jax.random.split(jax.random.fold_in(seeds[4], part), 5)
    return {
        "features": bell_draw(own_keys[0], (ROWS, NEURONS), 1.0, 6.0, ((0, 8), (1, 2))),
        "weights": bell_draw(seeds[1], (LAYER_TOTAL, 2, NBH, CAND, BLOCK, BLOCK), (2 * BLOCK) ** -0.5, 0.25, ((1, 2), (2, 8))),
        "active": plant((jax.random.randint(seeds[2], (LAYER_TOTAL, 2, NBH, CAND), 0, 3) < 2).astype(jnp.int32), jax.random.fold_in(seeds[2], 1), 0, 1),
        "layer_bias": jnp.clip(-0.5 + 0.8 * jax.random.uniform(seeds[3], (LAYER_TOTAL, 2, NBH, BLOCK), jnp.float32) ** steps_of(seeds[3], (LAYER_TOTAL, 2, NBH, BLOCK), ((1, 2), (2, 8)), -0.2, 0.2), -0.5, 0.3),
    }


def reference(features, weights, active, layer_bias):
    rows_all = features.shape[0]
    current_activation = features
    for layer_position in range(LAYER_TOTAL):
        blocked = current_activation.reshape(rows_all, 2, NBH, BLOCK).astype(jnp.float32)
        running_sum = jnp.zeros((rows_all, 2, NBH, BLOCK), jnp.float32)
        for source_position in range(2 * REACH + 2):
            if source_position < 2 * REACH + 1:
                source = jnp.roll(blocked, REACH - source_position, axis=2)
            else:
                source = blocked[:, ::-1]
            weight_now = weights[layer_position, :, :, source_position].astype(jnp.float32)
            keeping = active[layer_position, :, :, source_position] > 0
            weight_now = jnp.where(keeping[:, :, None, None], weight_now, jnp.float32(0.0))
            running_sum = running_sum + jnp.einsum("rhib,hibo->rhio", source, weight_now)
        running_sum = running_sum + layer_bias[layer_position][None]
        current_activation = jnp.maximum(running_sum, jnp.float32(0.0)).astype(jnp.bfloat16).reshape(rows_all, NEURONS)
    return current_activation
```

```python
import jax
import jax.numpy as jnp
from jax import lax
from jax.sharding import PartitionSpec as P


def shifted(block, axis, distance):
    size = lax.axis_size(axis)
    return lax.ppermute(block, axis, [((i + distance) % size, i) for i in range(size)])


def partner(block):
    return lax.ppermute(block, "cols", [(i, i ^ 1) for i in range(lax.axis_size("cols"))])


def neuron_layer(sources, weight_set, active_set, bias_row):
    kept = [jnp.where(active_set[m] > 0, source, jnp.zeros_like(source)) for m, source in enumerate(sources)]
    stacked = jnp.concatenate(kept, axis=1)
    total = jnp.dot(stacked, weight_set.reshape(-1, weight_set.shape[-1]), preferred_element_type=jnp.float32)
    return jnp.maximum(total + bias_row[None, :], 0.0).astype(jnp.bfloat16)


def on_device(features, weights, active, layer_bias):
    layer_count, _, _, candidates, width, _ = weights.shape
    reach = (candidates - 2) // 2
    devices = lax.axis_size("rows")
    samples = features.shape[0]

    blocks = features.reshape(samples, devices, width).transpose(1, 0, 2)
    spread = jnp.concatenate([jnp.roll(blocks, reach - m, axis=0) for m in range(2 * reach + 1)], axis=2)
    spread = lax.all_to_all(spread, "rows", split_axis=0, concat_axis=0, tiled=True)
    spread = spread.reshape(devices * samples, (2 * reach + 1) * width)
    sources = [spread[:, m * width : (m + 1) * width] for m in range(2 * reach + 1)]
    sources.append(partner(sources[reach]))
    for layer in range(layer_count):
        if layer:
            sources = [block if m == reach else shifted(block, "rows", m - reach) for m in range(2 * reach + 1)]
            sources.append(partner(block))
        block = neuron_layer(sources, weights[layer, 0, 0], active[layer, 0, 0], layer_bias[layer, 0, 0])
    return lax.all_to_all(block, "rows", split_axis=0, concat_axis=1, tiled=True)


def solution(mesh):
    in_specs = (
        P(("groups", "rows"), "cols"),
        P(None, "cols", "rows", None, None, None),
        P(None, "cols", "rows", None),
        P(None, "cols", "rows", None),
    )
    out_specs = P(("groups", "rows"), "cols")
    return jax.shard_map(
        on_device, mesh=mesh, in_specs=in_specs, out_specs=out_specs, check_vma=False
    )
```

```python
import functools

import jax
import jax.numpy as jnp
from jax import lax
from jax.experimental import pallas as pl
from jax.experimental.pallas import tpu as pltpu
from jax.sharding import PartitionSpec as P


def shifted(block, axis, distance):
    size = lax.axis_size(axis)
    return lax.ppermute(block, axis, [((i + distance) % size, i) for i in range(size)])


def partner(block):
    return lax.ppermute(block, "cols", [(i, i ^ 1) for i in range(lax.axis_size("cols"))])


def expand_kernel(reach, width, x_ref, o_ref):
    devices = o_ref.shape[0]
    for d in range(devices):
        for m in range(2 * reach + 1):
            source = (d + m - reach) % devices
            o_ref[d, :, m * width : (m + 1) * width] = x_ref[:, source * width : (source + 1) * width]


def expanded(features, devices, reach):
    samples, columns = features.shape
    width = columns // devices
    return pl.pallas_call(
        functools.partial(expand_kernel, reach, width),
        out_shape=jax.ShapeDtypeStruct((devices, samples, (2 * reach + 1) * width), features.dtype),
        in_specs=[pl.BlockSpec(memory_space=pltpu.VMEM)],
        out_specs=pl.BlockSpec(memory_space=pltpu.VMEM),
    )(features)


def neuron_layer(sources, weight_set, bias_row):
    stacked = jnp.concatenate(sources, axis=1)
    total = jnp.dot(stacked, weight_set, preferred_element_type=jnp.float32)
    return jnp.maximum(total + bias_row[None, :], 0.0).astype(jnp.bfloat16)


def on_device(features, weights, active, layer_bias):
    layer_count, _, _, candidates, width, _ = weights.shape
    reach = (candidates - 2) // 2
    devices = lax.axis_size("rows")
    samples = features.shape[0]

    spread = lax.all_to_all(expanded(features, devices, reach), "rows", split_axis=0, concat_axis=0, tiled=True)
    keep = active[:, 0, 0, :, None, None] > 0
    masked = jnp.where(keep, weights[:, 0, 0], jnp.zeros((), weights.dtype))
    masked = lax.optimization_barrier(masked.reshape(layer_count, candidates * width, width))

    spread = spread.reshape(devices * samples, (2 * reach + 1) * width)
    sources = [spread, partner(spread[:, reach * width : (reach + 1) * width])]
    order = [sign * step for sign in (1, -1) for step in range(reach, 0, -1)]
    for layer in range(layer_count):
        if layer:
            arrived = {0: block, None: partner(block)}
            for step in order:
                arrived[step] = shifted(block, "rows", step)
            sources = [arrived[m] for m in range(-reach, reach + 1)] + [arrived[None]]
        block = neuron_layer(sources, masked[layer], layer_bias[layer, 0, 0])
    return lax.all_to_all(block, "rows", split_axis=0, concat_axis=1, tiled=True)


def solution(mesh):
    in_specs = (
        P(("groups", "rows"), "cols"),
        P(None, "cols", "rows", None, None, None),
        P(None, "cols", "rows", None),
        P(None, "cols", "rows", None),
    )
    out_specs = P(("groups", "rows"), "cols")
    return jax.shard_map(
        on_device, mesh=mesh, in_specs=in_specs, out_specs=out_specs, check_vma=False
    )
```

```python
import functools

import jax
import jax.numpy as jnp
import numpy as np
from jax import lax
from jax.experimental import pallas as pl
from jax.experimental.pallas import tpu as pltpu
from jax.sharding import PartitionSpec as P


FAR, NEAR = 0, 1


def step_to(cycle, core, r, rows, where):
    if cycle == FAR:
        before = where(r <= 1, -2, where(r == rows - 1, 1, -1))
        after = where(r == 0, -1, where(r >= rows - 2, 2, 1))
    else:
        even = r % 2 == 0
        before = where(even, where(r == 0, 1, -2), where(r == rows - 1, -1, 2))
        after = where(even, where(r == rows - 2, 1, 2), where(r == 1, -1, -2))
    return where(core == 0, before, after)


def from_source(value, cycle):
    rows, cols = lax.axis_size("rows"), lax.axis_size("cols")
    pairs = []
    for r in range(rows):
        for c in range(cols):
            source = (r + int(step_to(cycle, c, r, rows, np.where))) % rows
            pairs.append((source * cols + c, r * cols + c))
    return lax.ppermute(value, ("rows", "cols"), pairs)


def partner(value):
    return lax.ppermute(value, "cols", [(i, i ^ 1) for i in range(lax.axis_size("cols"))])


def expand_kernel(reach, width, x_ref, o_ref):
    rows = o_ref.shape[0]
    for r in range(rows):
        for m in range(2 * reach + 1):
            source = (r + m - reach) % rows
            o_ref[r, :, m * width : (m + 1) * width] = x_ref[:, source * width : (source + 1) * width]


def expanded(features, rows, reach):
    samples, columns = features.shape
    width = columns // rows
    return pl.pallas_call(
        functools.partial(expand_kernel, reach, width),
        out_shape=pltpu.VMEM((rows, samples, (2 * reach + 1) * width), features.dtype),
        in_specs=[pl.BlockSpec(memory_space=pltpu.VMEM)],
        out_specs=pl.BlockSpec(memory_space=pltpu.VMEM),
    )(features)


def weight_kernel(plan, rows, active_ref, w_ref, *refs):
    outs, arrived = refs[:-1], refs[-1]
    width = w_ref.shape[-1]
    core, row = lax.axis_index("cols"), lax.axis_index("rows")
    copies = []
    for out, layer, sources in plan:
        for place, source in enumerate(sources):
            m = source(core, row)
            target = outs[out].at[pl.ds(place * width, width), :]
            copy = pltpu.make_async_copy(w_ref.at[layer, m], target, arrived.at[len(copies)])
            copy.start()
            copies.append((copy, layer, m, target))
    for copy, layer, m, target in copies:
        copy.wait()

        @pl.when(active_ref[layer, m] == 0)
        def _():
            target[...] = jnp.zeros_like(target)


def kept_weights(weights, active, reach, rows):
    layer_count, candidates, width, _ = weights.shape
    fixed = lambda m: lambda core, row: m
    taken = lambda cycle: lambda core, row: reach + step_to(cycle, core, row, rows, jnp.where)
    given = lambda cycle: lambda core, row: reach + step_to(cycle, 1 - core, row, rows, jnp.where)
    cycles = (FAR, NEAR)
    plan = [(0, 0, [fixed(m) for m in range(candidates - 1)]), (1, 0, [fixed(candidates - 1)])]
    for layer in range(1, layer_count):
        plan.append((len(plan), layer, [given(cycle) for cycle in cycles]))
        plan.append((len(plan), layer, [fixed(reach), fixed(candidates - 1)] + [taken(cycle) for cycle in cycles]))
    blocks = sum(len(sources) for _, _, sources in plan)
    return pl.pallas_call(
        functools.partial(weight_kernel, plan, rows),
        out_shape=[pltpu.VMEM((len(sources) * width, width), weights.dtype) for _, _, sources in plan],
        in_specs=[pl.BlockSpec(memory_space=pltpu.SMEM), pl.BlockSpec(memory_space=pl.ANY)],
        out_specs=[pl.BlockSpec(memory_space=pltpu.VMEM) for _ in plan],
        scratch_shapes=[pltpu.SemaphoreType.DMA((blocks,))],
        cost_estimate=pl.CostEstimate(flops=0, bytes_accessed=2 * weights.size * 2, transcendentals=0),
    )(active, weights)


def on_device(features, weights, active, layer_bias):
    layer_count, _, _, candidates, width, _ = weights.shape
    reach = (candidates - 2) // 2
    rows, cols = lax.axis_size("rows"), lax.axis_size("cols")
    core = lax.axis_index("cols")
    samples = features.shape[0]

    spread = lax.all_to_all(expanded(features, rows, reach), "rows", split_axis=0, concat_axis=0, tiled=True)
    kept = kept_weights(weights[:, 0, 0], active[:, 0, 0], reach, rows)
    for_own = kept[0:1] + kept[3::2]
    for_other = [partner(w) for w in kept[1:2] + kept[2::2]]

    spread = spread.reshape(rows * samples, (2 * reach + 1) * width)
    for layer in range(layer_count):
        if layer:
            both = jnp.concatenate([own, other], axis=1)
            again = lax.optimization_barrier(jnp.concatenate(lax.optimization_barrier([own, other]), axis=1))
            arrived = [both, from_source(both, FAR), from_source(again, NEAR)]
            own, other = [x[:, :width] for x in arrived], [x[:, width:] for x in arrived]
            to_own = jnp.concatenate([own[0], other[0]] + own[1:], axis=1)
            to_other = jnp.concatenate(other[1:], axis=1)
        else:
            to_own, to_other = spread, spread[:, reach * width : (reach + 1) * width]
        part_own = jnp.dot(to_own, for_own[layer], preferred_element_type=jnp.float32)
        part_own = part_own + layer_bias[layer, 0, 0][None, :]
        part_other = jnp.dot(to_other, for_other[layer], preferred_element_type=jnp.float32)
        if layer < layer_count - 1:
            far = partner(jnp.concatenate([part_own, part_other], axis=1))
            own = jnp.maximum(part_own + far[:, width:], 0.0).astype(jnp.bfloat16)
            other = jnp.maximum(part_other + far[:, :width], 0.0).astype(jnp.bfloat16)
    shape = (rows, samples, width)
    by_half = [jnp.where(core == h, part_own, part_other).reshape(shape) for h in range(cols)]
    parts = jnp.stack(by_half, axis=1).reshape(rows * cols, samples, width)
    parts = lax.all_to_all(parts, ("rows", "cols"), split_axis=0, concat_axis=0, tiled=True)
    total = parts.reshape(rows, cols, samples, width).sum(axis=1)
    return jnp.maximum(total, 0.0).astype(jnp.bfloat16).transpose(1, 0, 2).reshape(samples, rows * width)


def solution(mesh):
    in_specs = (
        P(("groups", "rows"), "cols"),
        P(None, "cols", "rows", None, None, None),
        P(None, "cols", "rows", None),
        P(None, "cols", "rows", None),
    )
    out_specs = P(("groups", "rows"), "cols")
    return jax.shard_map(
        on_device, mesh=mesh, in_specs=in_specs, out_specs=out_specs, check_vma=False
    )
```

```python
import functools

import jax
import jax.numpy as jnp
import numpy as np
from jax import lax
from jax.experimental import pallas as pl
from jax.experimental.pallas import tpu as pltpu
from jax.sharding import PartitionSpec as P


FAR, NEAR = 0, 1


def step_to(cycle, core, r, rows, where):
    even = r % 2 == 0
    first, last = r <= 1, r >= rows - 2
    if cycle == FAR:
        on_core_0 = where(first, -2, where(last, 2, where(even, 1, -1)))
        on_core_1 = where(even, -1, 1)
    else:
        on_core_0 = where(first | last, where(even, 1, -1), where(r % 4 < 2, -2, 2))
        on_core_1 = where(r % 4 < 2, 2, -2)
    return where(core == 0, on_core_0, on_core_1)


def from_source(value, cycle):
    rows, cols = lax.axis_size("rows"), lax.axis_size("cols")
    pairs = []
    for r in range(rows):
        for c in range(cols):
            source = (r + int(step_to(cycle, c, r, rows, np.where))) % rows
            pairs.append((source * cols + c, r * cols + c))
    return lax.ppermute(value, ("rows", "cols"), pairs)


def partner(value):
    return lax.ppermute(value, "cols", [(i, i ^ 1) for i in range(lax.axis_size("cols"))])


def expand_kernel(reach, width, x_ref, o_ref):
    rows = o_ref.shape[0]
    for r in range(rows):
        for m in range(2 * reach + 1):
            source = (r + m - reach) % rows
            o_ref[r, :, m * width : (m + 1) * width] = x_ref[:, source * width : (source + 1) * width]


def expanded(features, rows, reach):
    samples, columns = features.shape
    width = columns // rows
    return pl.pallas_call(
        functools.partial(expand_kernel, reach, width),
        out_shape=pltpu.VMEM((rows, samples, (2 * reach + 1) * width), features.dtype),
        in_specs=[pl.BlockSpec(memory_space=pltpu.VMEM)],
        out_specs=pl.BlockSpec(memory_space=pltpu.VMEM),
    )(features)


def weight_kernel(plan, rows, active_ref, w_ref, *refs):
    outs, arrived = refs[:-1], refs[-1]
    width = w_ref.shape[-1]
    core, row = lax.axis_index("cols"), lax.axis_index("rows")
    copies = []
    for out, layer, sources in plan:
        for place, source in enumerate(sources):
            m = source(core, row)
            target = outs[out].at[pl.ds(place * width, width), :]
            copy = pltpu.make_async_copy(w_ref.at[layer, m], target, arrived.at[len(copies)])
            copy.start()
            copies.append((copy, layer, m, target))
    for copy, layer, m, target in copies:
        copy.wait()

        @pl.when(active_ref[layer, m] == 0)
        def _():
            target[...] = jnp.zeros_like(target)


def kept_weights(weights, active, reach, rows):
    layer_count, candidates, width, _ = weights.shape
    fixed = lambda m: lambda core, row: m
    taken = lambda cycle: lambda core, row: reach + step_to(cycle, core, row, rows, jnp.where)
    given = lambda cycle: lambda core, row: reach + step_to(cycle, 1 - core, row, rows, jnp.where)
    cycles = (FAR, NEAR)
    plan = [(0, 0, [fixed(m) for m in range(candidates - 1)]), (1, 0, [fixed(candidates - 1)])]
    for layer in range(1, layer_count):
        plan.append((len(plan), layer, [given(cycle) for cycle in cycles]))
        plan.append((len(plan), layer, [fixed(reach), fixed(candidates - 1)] + [taken(cycle) for cycle in cycles]))
    blocks = sum(len(sources) for _, _, sources in plan)
    return pl.pallas_call(
        functools.partial(weight_kernel, plan, rows),
        out_shape=[pltpu.VMEM((len(sources) * width, width), weights.dtype) for _, _, sources in plan],
        in_specs=[pl.BlockSpec(memory_space=pltpu.SMEM), pl.BlockSpec(memory_space=pl.ANY)],
        out_specs=[pl.BlockSpec(memory_space=pltpu.VMEM) for _ in plan],
        scratch_shapes=[pltpu.SemaphoreType.DMA((blocks,))],
        cost_estimate=pl.CostEstimate(flops=0, bytes_accessed=2 * weights.size * 2, transcendentals=0),
    )(active, weights)


def on_device(features, weights, active, layer_bias):
    layer_count, _, _, candidates, width, _ = weights.shape
    reach = (candidates - 2) // 2
    rows, cols = lax.axis_size("rows"), lax.axis_size("cols")
    core = lax.axis_index("cols")
    samples = features.shape[0]

    spread = lax.all_to_all(expanded(features, rows, reach), "rows", split_axis=0, concat_axis=0, tiled=True)
    kept = kept_weights(weights[:, 0, 0], active[:, 0, 0], reach, rows)
    for_own = kept[0:1] + kept[3::2]
    for_other = [partner(w) for w in kept[1:2] + kept[2::2]]

    spread = spread.reshape(rows * samples, (2 * reach + 1) * width)
    for layer in range(layer_count):
        if layer:
            both = jnp.concatenate([own, other], axis=1)
            again = lax.optimization_barrier(jnp.concatenate(lax.optimization_barrier([own, other]), axis=1))
            arrived = [both, from_source(both, FAR), from_source(again, NEAR)]
            own, other = [x[:, :width] for x in arrived], [x[:, width:] for x in arrived]
            to_own = jnp.concatenate([own[0], other[0]] + own[1:], axis=1)
            to_other = jnp.concatenate(other[1:], axis=1)
        else:
            to_own, to_other = spread, spread[:, reach * width : (reach + 1) * width]
        part_own = jnp.dot(to_own, for_own[layer], preferred_element_type=jnp.float32)
        part_own = part_own + layer_bias[layer, 0, 0][None, :]
        part_other = jnp.dot(to_other, for_other[layer], preferred_element_type=jnp.float32)
        if layer < layer_count - 1:
            far = partner(jnp.concatenate([part_own, part_other], axis=1))
            own = jnp.maximum(part_own + far[:, width:], 0.0).astype(jnp.bfloat16)
            other = jnp.maximum(part_other + far[:, :width], 0.0).astype(jnp.bfloat16)
    shape = (rows, samples, width)
    by_half = [jnp.where(core == h, part_own, part_other).reshape(shape) for h in range(cols)]
    parts = jnp.stack(by_half, axis=1).reshape(rows * cols, samples, width)
    parts = lax.all_to_all(parts, ("rows", "cols"), split_axis=0, concat_axis=0, tiled=True)
    total = parts.reshape(rows, cols, samples, width).sum(axis=1)
    return jnp.maximum(total, 0.0).astype(jnp.bfloat16).transpose(1, 0, 2).reshape(samples, rows * width)


def solution(mesh):
    in_specs = (
        P(("groups", "rows"), "cols"),
        P(None, "cols", "rows", None, None, None),
        P(None, "cols", "rows", None),
        P(None, "cols", "rows", None),
    )
    out_specs = P(("groups", "rows"), "cols")
    return jax.shard_map(
        on_device, mesh=mesh, in_specs=in_specs, out_specs=out_specs, check_vma=False
    )
```

```python
import functools

import jax
import jax.numpy as jnp
import numpy as np
from jax import lax
from jax.experimental import pallas as pl
from jax.experimental.pallas import tpu as pltpu
from jax.sharding import PartitionSpec as P


FAR, NEAR = 0, 1


def step_to(cycle, core, r, rows, where):
    even = r % 2 == 0
    first, last = r <= 1, r >= rows - 2
    if cycle == FAR:
        on_core_0 = where(first, -2, where(last, 2, where(even, 1, -1)))
        on_core_1 = where(even, -1, 1)
    else:
        on_core_0 = where(first | last, where(even, 1, -1), where(r % 4 < 2, -2, 2))
        on_core_1 = where(r % 4 < 2, 2, -2)
    return where(core == 0, on_core_0, on_core_1)


def from_source(value, cycle):
    rows, cols = lax.axis_size("rows"), lax.axis_size("cols")
    pairs = []
    for r in range(rows):
        for c in range(cols):
            source = (r + int(step_to(cycle, c, r, rows, np.where))) % rows
            pairs.append((source * cols + c, r * cols + c))
    return lax.ppermute(value, ("rows", "cols"), pairs)


def partner(value):
    return lax.ppermute(value, "cols", [(i, i ^ 1) for i in range(lax.axis_size("cols"))])


def in_turns(rows):
    return [p // 2 if p % 2 == 0 else rows - 1 - p // 2 for p in range(rows)]


def expand_kernel(reach, width, x_ref, o_ref):
    rows = o_ref.shape[0]
    for p, r in enumerate(in_turns(rows)):
        for m in range(2 * reach + 1):
            source = (r + m - reach) % rows
            o_ref[p, :, m * width : (m + 1) * width] = x_ref[:, source * width : (source + 1) * width]


def expanded(features, rows, reach):
    samples, columns = features.shape
    width = columns // rows
    return pl.pallas_call(
        functools.partial(expand_kernel, reach, width),
        out_shape=pltpu.VMEM((rows, samples, (2 * reach + 1) * width), features.dtype),
        in_specs=[pl.BlockSpec(memory_space=pltpu.VMEM)],
        out_specs=pl.BlockSpec(memory_space=pltpu.VMEM),
    )(features)


def weight_kernel(plan, rows, active_ref, w_ref, *refs):
    outs, arrived = refs[:-1], refs[-1]
    width = w_ref.shape[-1]
    core, row = lax.axis_index("cols"), lax.axis_index("rows")
    copies = []
    for out, layer, sources in plan:
        for place, source in enumerate(sources):
            m = source(core, row)
            target = outs[out].at[pl.ds(place * width, width), :]
            copy = pltpu.make_async_copy(w_ref.at[layer, m], target, arrived.at[len(copies)])
            copy.start()
            copies.append((copy, layer, m, target))
    for copy, layer, m, target in copies:
        copy.wait()

        @pl.when(active_ref[layer, m] == 0)
        def _():
            target[...] = jnp.zeros_like(target)


def kept_weights(weights, active, reach, rows):
    layer_count, candidates, width, _ = weights.shape
    fixed = lambda m: lambda core, row: m
    taken = lambda cycle: lambda core, row: reach + step_to(cycle, core, row, rows, jnp.where)
    given = lambda cycle: lambda core, row: reach + step_to(cycle, 1 - core, row, rows, jnp.where)
    cycles = (FAR, NEAR)
    plan = [(0, 0, [fixed(m) for m in range(candidates - 1)]), (1, 0, [fixed(candidates - 1)])]
    for layer in range(1, layer_count):
        plan.append((len(plan), layer, [given(cycle) for cycle in cycles]))
        plan.append((len(plan), layer, [fixed(reach), fixed(candidates - 1)] + [taken(cycle) for cycle in cycles]))
    blocks = sum(len(sources) for _, _, sources in plan)
    return pl.pallas_call(
        functools.partial(weight_kernel, plan, rows),
        out_shape=[pltpu.VMEM((len(sources) * width, width), weights.dtype) for _, _, sources in plan],
        in_specs=[pl.BlockSpec(memory_space=pltpu.SMEM), pl.BlockSpec(memory_space=pl.ANY)],
        out_specs=[pl.BlockSpec(memory_space=pltpu.VMEM) for _ in plan],
        scratch_shapes=[pltpu.SemaphoreType.DMA((blocks,))],
        cost_estimate=pl.CostEstimate(flops=0, bytes_accessed=2 * weights.size * 2, transcendentals=0),
    )(active, weights)


def on_device(features, weights, active, layer_bias):
    layer_count, _, _, candidates, width, _ = weights.shape
    reach = (candidates - 2) // 2
    rows, cols = lax.axis_size("rows"), lax.axis_size("cols")
    core = lax.axis_index("cols")
    samples = features.shape[0]

    axes, turns = ("rows", "cols"), in_turns(rows)
    halves = [[r * cols + c for r in turns] for c in range(cols)]
    spread = lax.all_to_all(expanded(features, rows, reach), axes, 0, 0, axis_index_groups=halves, tiled=True)
    kept = kept_weights(weights[:, 0, 0], active[:, 0, 0], reach, rows)
    for_own = kept[0:1] + kept[3::2]
    for_other = [partner(w) for w in kept[1:2] + kept[2::2]]

    spread = spread.reshape(rows * samples, (2 * reach + 1) * width)
    for layer in range(layer_count):
        if layer:
            both = jnp.concatenate([own, other], axis=1)
            again = lax.optimization_barrier(jnp.concatenate(lax.optimization_barrier([own, other]), axis=1))
            arrived = [both, from_source(both, FAR), from_source(again, NEAR)]
            own, other = [x[:, :width] for x in arrived], [x[:, width:] for x in arrived]
            to_own = jnp.concatenate([own[0], other[0]] + own[1:], axis=1)
            to_other = jnp.concatenate(other[1:], axis=1)
        else:
            to_own, to_other = spread, spread[:, reach * width : (reach + 1) * width]
        part_own = jnp.dot(to_own, for_own[layer], preferred_element_type=jnp.float32)
        part_own = part_own + layer_bias[layer, 0, 0][None, :]
        part_other = jnp.dot(to_other, for_other[layer], preferred_element_type=jnp.float32)
        if layer < layer_count - 1:
            far = partner(jnp.concatenate([part_own, part_other], axis=1))
            own = jnp.maximum(part_own + far[:, width:], 0.0).astype(jnp.bfloat16)
            other = jnp.maximum(part_other + far[:, :width], 0.0).astype(jnp.bfloat16)
    shape = (rows, samples, width)
    by_half = [jnp.where(core == h, part_own, part_other).reshape(shape) for h in range(cols)]
    parts = jnp.stack(by_half, axis=1).reshape(rows * cols, samples, width)
    everyone = [[r * cols + c for r in turns for c in range(cols)]]
    parts = lax.all_to_all(parts, axes, 0, 0, axis_index_groups=everyone, tiled=True)
    total = parts.reshape(rows, cols, samples, width).sum(axis=1)
    block = jnp.maximum(total, 0.0).astype(jnp.bfloat16)
    block = jnp.concatenate([block[0::2], block[1::2][::-1]], axis=0)
    return block.transpose(1, 0, 2).reshape(samples, rows * width)


def solution(mesh):
    in_specs = (
        P(("groups", "rows"), "cols"),
        P(None, "cols", "rows", None, None, None),
        P(None, "cols", "rows", None),
        P(None, "cols", "rows", None),
    )
    out_specs = P(("groups", "rows"), "cols")
    return jax.shard_map(
        on_device, mesh=mesh, in_specs=in_specs, out_specs=out_specs, check_vma=False
    )
```

```python
import functools

import jax
import jax.numpy as jnp
import numpy as np
from jax import lax
from jax.experimental import pallas as pl
from jax.experimental.pallas import tpu as pltpu
from jax.sharding import PartitionSpec as P


FAR, NEAR = 0, 1


def step_to(cycle, core, r, rows, where):
    even = r % 2 == 0
    first, last = r <= 1, r >= rows - 2
    if cycle == FAR:
        on_core_0 = where(first, -2, where(last, 2, where(even, 1, -1)))
        on_core_1 = where(even, -1, 1)
    else:
        on_core_0 = where(first | last, where(even, 1, -1), where(r % 4 < 2, -2, 2))
        on_core_1 = where(r % 4 < 2, 2, -2)
    return where(core == 0, on_core_0, on_core_1)


def from_source(value, cycle):
    rows, cols = lax.axis_size("rows"), lax.axis_size("cols")
    pairs = []
    for r in range(rows):
        for c in range(cols):
            source = (r + int(step_to(cycle, c, r, rows, np.where))) % rows
            pairs.append((source * cols + c, r * cols + c))
    return lax.ppermute(value, ("rows", "cols"), pairs)


def partner(value):
    return lax.ppermute(value, "cols", [(i, i ^ 1) for i in range(lax.axis_size("cols"))])


def in_turns(rows):
    return [p // 2 if p % 2 == 0 else rows - 1 - p // 2 for p in range(rows)]


def expand_kernel(reach, width, x_ref, o_ref):
    rows = o_ref.shape[0]
    for p, r in enumerate(in_turns(rows)):
        for m in range(2 * reach + 1):
            source = (r + m - reach) % rows
            o_ref[p, :, m * width : (m + 1) * width] = x_ref[:, source * width : (source + 1) * width]


def expanded(features, rows, reach):
    samples, columns = features.shape
    width = columns // rows
    return pl.pallas_call(
        functools.partial(expand_kernel, reach, width),
        out_shape=pltpu.VMEM((rows, samples, (2 * reach + 1) * width), features.dtype),
        in_specs=[pl.BlockSpec(memory_space=pltpu.VMEM)],
        out_specs=pl.BlockSpec(memory_space=pltpu.VMEM),
    )(features)


def weight_kernel(plan, rows, active_ref, w_ref, *refs):
    outs, arrived = refs[:-1], refs[-1]
    width = w_ref.shape[-1]
    core, row = lax.axis_index("cols"), lax.axis_index("rows")
    copies = []
    for out, layer, sources in plan:
        for place, source in enumerate(sources):
            m = source(core, row)
            target = outs[out].at[pl.ds(place * width, width), :]
            copy = pltpu.make_async_copy(w_ref.at[layer, m], target, arrived.at[len(copies)])
            copy.start()
            copies.append((copy, layer, m, target))
    for copy, layer, m, target in copies:
        copy.wait()

        @pl.when(active_ref[layer, m] == 0)
        def _():
            target[...] = jnp.zeros_like(target)


def kept_weights(weights, active, reach, rows):
    layer_count, candidates, width, _ = weights.shape
    fixed = lambda m: lambda core, row: m
    taken = lambda cycle: lambda core, row: reach + step_to(cycle, core, row, rows, jnp.where)
    given = lambda cycle: lambda core, row: reach + step_to(cycle, 1 - core, row, rows, jnp.where)
    cycles = (FAR, NEAR)
    plan = [(0, 0, [fixed(m) for m in range(candidates - 1)]), (1, 0, [fixed(candidates - 1)])]
    for layer in range(1, layer_count):
        plan.append((len(plan), layer, [given(cycle) for cycle in cycles]))
        plan.append((len(plan), layer, [fixed(reach), fixed(candidates - 1)] + [taken(cycle) for cycle in cycles]))
    blocks = sum(len(sources) for _, _, sources in plan)
    return pl.pallas_call(
        functools.partial(weight_kernel, plan, rows),
        out_shape=[pltpu.VMEM((len(sources) * width, width), weights.dtype) for _, _, sources in plan],
        in_specs=[pl.BlockSpec(memory_space=pltpu.SMEM), pl.BlockSpec(memory_space=pl.ANY)],
        out_specs=[pl.BlockSpec(memory_space=pltpu.VMEM) for _ in plan],
        scratch_shapes=[pltpu.SemaphoreType.DMA((blocks,))],
        cost_estimate=pl.CostEstimate(flops=0, bytes_accessed=2 * weights.size * 2, transcendentals=0),
    )(active, weights)


def layer_kernel(both_ref, far_ref, near_ref, own_w_ref, other_w_ref, bias_ref, o_ref):
    width = bias_ref.shape[-1]
    first, second = slice(0, width), slice(width, 2 * width)
    dot = functools.partial(jnp.dot, preferred_element_type=jnp.float32)
    own_parts = [both_ref[:, first], both_ref[:, second], far_ref[:, first], near_ref[:, first]]
    own = bias_ref[...]
    for k, part in enumerate(own_parts):
        own = own + dot(part, own_w_ref[k * width : (k + 1) * width, :])
    other = dot(far_ref[:, second], other_w_ref[first, :]) + dot(near_ref[:, second], other_w_ref[second, :])
    if len(o_ref.shape) == 2:
        o_ref[:, first], o_ref[:, second] = own, other
    else:
        core, samples = lax.axis_index("cols"), o_ref.shape[2]
        for p in range(o_ref.shape[0]):
            o_ref[p, core] = own[p * samples : (p + 1) * samples]
            o_ref[p, 1 - core] = other[p * samples : (p + 1) * samples]


def partial_sums(both, far, near, own_w, other_w, bias, shape):
    vmem = pl.BlockSpec(memory_space=pltpu.VMEM)
    flops = 2 * both.shape[0] * (own_w.size + other_w.size)
    return pl.pallas_call(
        layer_kernel,
        out_shape=pltpu.VMEM(shape, jnp.float32),
        in_specs=[vmem] * 6,
        out_specs=vmem,
        cost_estimate=pl.CostEstimate(flops=flops, bytes_accessed=2 * own_w.size, transcendentals=0),
    )(*(pltpu.with_memory_space_constraint(x, pltpu.VMEM) for x in (both, far, near, own_w, other_w, bias)))


def on_device(features, weights, active, layer_bias):
    layer_count, _, _, candidates, width, _ = weights.shape
    reach = (candidates - 2) // 2
    rows, cols = lax.axis_size("rows"), lax.axis_size("cols")
    samples = features.shape[0]

    axes, turns = ("rows", "cols"), in_turns(rows)
    halves = [[r * cols + c for r in turns] for c in range(cols)]
    spread = lax.all_to_all(expanded(features, rows, reach), axes, 0, 0, axis_index_groups=halves, tiled=True)
    kept = kept_weights(weights[:, 0, 0], active[:, 0, 0], reach, rows)
    for_own = kept[0:1] + kept[3::2]
    for_other = [partner(w) for w in kept[1:2] + kept[2::2]]

    spread = spread.reshape(rows * samples, (2 * reach + 1) * width)
    for layer in range(layer_count):
        if layer:
            both = jnp.concatenate([own, other], axis=1)
            again = lax.optimization_barrier(jnp.concatenate(lax.optimization_barrier([own, other]), axis=1))
            shape = both.shape if layer < layer_count - 1 else (rows, cols, samples, width)
            far_blocks, near_blocks = from_source(again, FAR), from_source(both, NEAR)
            bias = layer_bias[layer, 0]
            parts = partial_sums(both, far_blocks, near_blocks, for_own[layer], for_other[layer], bias, shape)
        else:
            part_own = jnp.dot(spread, for_own[layer], preferred_element_type=jnp.float32)
            part_own = part_own + layer_bias[layer, 0, 0][None, :]
            block = spread[:, reach * width : (reach + 1) * width]
            part_other = jnp.dot(block, for_other[layer], preferred_element_type=jnp.float32)
            parts = jnp.concatenate([part_own, part_other], axis=1)
        if layer < layer_count - 1:
            far = partner(parts)
            own = jnp.maximum(parts[:, :width] + far[:, width:], 0.0).astype(jnp.bfloat16)
            other = jnp.maximum(parts[:, width:] + far[:, :width], 0.0).astype(jnp.bfloat16)
    parts = parts.reshape(rows * cols, samples, width)
    everyone = [[r * cols + c for r in turns for c in range(cols)]]
    parts = lax.all_to_all(parts, axes, 0, 0, axis_index_groups=everyone, tiled=True)
    total = parts.reshape(rows, cols, samples, width).sum(axis=1)
    block = jnp.maximum(total, 0.0).astype(jnp.bfloat16)
    block = jnp.concatenate([block[0::2], block[1::2][::-1]], axis=0)
    return block.transpose(1, 0, 2).reshape(samples, rows * width)


def solution(mesh):
    in_specs = (
        P(("groups", "rows"), "cols"),
        P(None, "cols", "rows", None, None, None),
        P(None, "cols", "rows", None),
        P(None, "cols", "rows", None),
    )
    out_specs = P(("groups", "rows"), "cols")
    return jax.shard_map(
        on_device, mesh=mesh, in_specs=in_specs, out_specs=out_specs, check_vma=False
    )
```
